256 devices in a mesh: freq: 4 (over y), tile: 64 (over z, x, core).
Axes of the slice: x: 4, y: 4, z: 8, core: 2. Of those that a mesh axis runs over, the one named last changes fastest.
Arguments:
- traces: bfloat16 [256, 8192, 128], P('freq', 'tile'), may hold values from -6 to 6
- right_basis: bfloat16 [16, 8192, 4096], P('freq', 'tile'), may hold values from -0.25 to 0.25
- left_basis: bfloat16 [16, 8192, 4096], P('freq', 'tile'), may hold values from -0.09375 to 0.09375
- tile_ranks: int32 [16, 32, 32], P('freq'), may hold values from 8 to 64, as said below
Outputs:
- wavefield: bfloat16 [16, 2, 8192, 128], P('freq', None, 'tile')
The draws below stay inside these ranges and needn't reach their ends.
Inputs may be any that keep to these rules, and one draw needn't show every extreme that they name: `tile_ranks`: diagonal tiles have rank 64; the ranks of the other tiles are drawn independently of the tile's position, evenly over the whole range.
All inputs are finite; a program needn't handle non-finite values.
Results may differ from the reference program's by a relative error of at most 0.015.
Values may be sent and summed in bfloat16 or wider, within the bound.
No kernel may reach another device: no remote copies, remote signals or barrier semaphores. Data moves between devices by JAX's collectives and lax.ppermute only.
A program may use at most 128 MiB of HBM per device.

```python
import math
import jax
import jax.numpy as jnp
from jax import lax

N = 8192
TB = 256
R = 64
S = 128
NF = 16
NT = 256
NB = 32
N_TILE = 64


def draw_tile_ranks(key, part):
    tile_index = jnp.arange(NB, dtype=jnp.int32)
    lowest = max(R // 8, 1)
    rank_value = jax.random.randint(key, (NF, NB, NB), lowest, R + 1, dtype=jnp.int32)
    on_diagonal = tile_index[:, None] == tile_index[None, :]
    rank_value = jnp.where(on_diagonal[None], R, rank_value)
    return rank_value.astype(jnp.int32)


def shard_levels(key, shape, pieces, least, high):
    factor_of, own = 1.0, jax.random.fold_in(key, 6)
    for position, blocks in pieces:
        heights = jnp.exp(jax.random.uniform(jax.random.fold_in(own, position), (blocks,), jnp.float32, least / len(pieces), high / len(pieces)))
        factor_of = factor_of * jnp.repeat(heights, shape[position] // blocks).reshape([-1 if axis == position else 1 for axis in range(len(shape))])
    return factor_of


def normal_values(rng, shape, scale, most, shards=(), kind=jnp.bfloat16):
    result = jax.random.normal(rng, shape, jnp.float32) * scale
    if len(shards) > 0:
        result = shard_levels(rng, shape, shards, -0.22, 0.18) * result
    return jnp.clip(result, min=-most, max=most).astype(kind)


def setup_inputs(seed: int = 0) -> dict:
    key_of = jax.random.split(jax.random.key(seed), 5)
    traces = normal_values(key_of[0], (NT, N, S), 1.0, 6.0, ((0, 4), (1, 64)))
    right_basis = normal_values(key_of[1], (NF, N, 2 * NB * R), (2 * TB) ** -0.5, 0.25, ((0, 4), (1, 64)))
    left_basis = normal_values(key_of[2], (NF, N, 2 * NB * R), (2 * NB * R) ** -0.5, 0.09375, ((0, 4), (1, 64)))
    tile_ranks = draw_tile_ranks(jax.random.fold_in(key_of[4], 71), 0)
    return dict(traces=traces, right_basis=right_basis, left_basis=left_basis, tile_ranks=tile_ranks)


def twiddles(freq_ids, time_ids, total_time):
    phase_int = freq_ids[:, None] * time_ids[None, :] % total_time
    angle_rad = phase_int.astype(jnp.float32) * (2.0 * math.pi / total_time)
    factor = 1.0 / math.sqrt(total_time)
    return jnp.stack([jnp.cos(angle_rad) * factor, -jnp.sin(angle_rad) * factor], 1).astype(jnp.bfloat16)

def reference(traces, right_basis, left_basis, tile_ranks):
    tile_rows = N // TB
    grid_rows = N // N_TILE
    piece_rows = min(TB, grid_rows)
    piece_count = N // piece_rows
    per_tile = max(TB // grid_rows, 1)
    flat_traces = traces.reshape(NT, N * S)
    time_ids = jnp.arange(NT, dtype=jnp.int32)
    column_ids = jnp.arange(piece_count, dtype=jnp.int32) // per_tile

    def one_freq(inputs):
        freq_index, right_freq, left_freq, ranks_freq = inputs
        twiddle = twiddles(jnp.reshape(freq_index + 1, (1,)).astype(jnp.int32), time_ids, NT)[0]
        spectra = jnp.dot(twiddle, flat_traces, preferred_element_type=jnp.float32).astype(jnp.bfloat16)
        spectra = spectra.reshape(2, piece_count, piece_rows, S)
        right_pieces = right_freq.reshape(piece_count, piece_rows, 2 * tile_rows * R)
        products = jnp.einsum('qnc,pqns->cqps', right_pieces.astype(jnp.float32), spectra.astype(jnp.float32))
        products = products.reshape(2, tile_rows, R, piece_count, 2, S)
        real_part = products[0, :, :, :, 0] - products[1, :, :, :, 1]
        imag_part = products[0, :, :, :, 1] + products[1, :, :, :, 0]
        stacked = jnp.transpose(jnp.stack([real_part, imag_part], 0), (3, 1, 0, 2, 4))
        chosen = ranks_freq[:, column_ids]
        keep_rows = jnp.arange(R, dtype=jnp.int32)[None, None, :] < jnp.transpose(chosen)[:, :, None]
        rank_rows = jnp.where(keep_rows[:, :, None, :, None], stacked, jnp.float32(0.0)).astype(jnp.bfloat16)
        grouped = rank_rows.astype(jnp.float32).reshape(tile_rows, per_tile, tile_rows, 2, R, S)
        coupled = lax.optimization_barrier(jnp.sum(grouped, axis=1)).astype(jnp.bfloat16)
        by_row = jnp.transpose(coupled, (1, 0, 2, 3, 4))
        real_coupled = by_row[:, :, 0]
        imag_coupled = by_row[:, :, 1]
        upper_half = jnp.stack([real_coupled, imag_coupled], -2)
        lower_half = jnp.stack([-imag_coupled, real_coupled], -2)
        operand = jnp.stack([upper_half, lower_half], 1)
        left_tiles = left_freq.reshape(tile_rows, TB, 2, tile_rows, R)
        field_out = jnp.einsum('itajk,iajkys->yits', left_tiles.astype(jnp.float32), operand.astype(jnp.float32))
        return field_out.reshape(2, N, S).astype(jnp.bfloat16)
    return lax.map(one_freq, (jnp.arange(NF, dtype=jnp.int32), right_basis, left_basis, tile_ranks))
```

```python
import math

import jax
import jax.numpy as jnp
import numpy as np
from jax import lax
from jax.experimental import pallas as pl
from jax.experimental.pallas import tpu as pltpu
from jax.sharding import Mesh
from jax.sharding import PartitionSpec as P

N = 8192
TB = 256
R = 64
S = 128
NF = 16
NT = 256
NB = 32
NY, NZ, NX, NC = 4, 8, 4, 2
TROWS = NT // NY
FDEV = NF // NY
BF = jnp.bfloat16
F32 = jnp.float32
GROUP = 16
VMEM = 48 * 1024 * 1024


def twiddle_blocks():
    k = np.arange(1, NF + 1)[:, None]
    t = np.arange(NT)[None, :]
    angle = ((k * t) % NT).astype(np.float32) * np.float32(2.0 * math.pi / NT)
    scale = np.float32(1.0 / math.sqrt(NT))
    tw = np.stack([np.cos(angle) * scale, -np.sin(angle) * scale], 1)
    tw = tw.reshape(NY, NC, 2, 2, NY, TROWS)
    out = np.zeros((NY, NY, 2, NC, 2, TROWS), np.float32)
    for y in range(NY):
        for d in range(NY):
            out[y, d] = np.transpose(tw[(y + d) % NY, :, :, :, y], (1, 0, 2, 3))
    out = out.reshape(NY, 32, TROWS)
    eye = np.eye(GROUP, dtype=np.float32)
    big = out[:, :, None, :, None] * eye[None, None, :, None, :]
    return big.reshape(NY, 32 * GROUP, TROWS * GROUP).astype(jnp.bfloat16)


def dft_kernel(ids, w_ref, t_ref, *outs):
    wide = t_ref.shape[1] // GROUP
    cols = [
        t_ref[:, g * GROUP : (g + 1) * GROUP, :].reshape(TROWS * GROUP, S) for g in range(wide)
    ]
    rhs = jnp.concatenate(cols, axis=1)
    acc = jnp.dot(w_ref[0], rhs, preferred_element_type=F32).astype(BF)
    per = 32 // len(outs)
    for o, ref in enumerate(outs):
        for j in range(per):
            row = (o * per + j) * GROUP
            for g in range(wide):
                ref[j // 4, (j // 2) % 2, j % 2, g * GROUP : (g + 1) * GROUP, :] = acc[
                    row : row + GROUP, g * S : (g + 1) * S
                ]


def dft(y, w, traces):
    rows = 32
    outs = NY
    return pl.pallas_call(
        dft_kernel,
        grid_spec=pltpu.PrefetchScalarGridSpec(
            num_scalar_prefetch=1,
            grid=(128 // rows,),
            in_specs=[
                pl.BlockSpec((1, 32 * GROUP, TROWS * GROUP), lambda i, ids: (ids[0], 0, 0)),
                pl.BlockSpec((TROWS, rows, S), lambda i, ids: (0, i, 0)),
            ],
            out_specs=[
                pl.BlockSpec((2, NC, 2, rows, S), lambda i, ids: (0, 0, 0, i, 0))
                for _ in range(outs)
            ],
        ),
        out_shape=[jax.ShapeDtypeStruct((2, NC, 2, 128, S), BF) for _ in range(outs)],
        compiler_params=pltpu.CompilerParams(vmem_limit_bytes=VMEM),
        cost_estimate=pl.CostEstimate(
            flops=2 * 512 * 1024 * 1024, bytes_accessed=5 << 20, transcendentals=0
        ),
    )(y, w, traces)


def sum_kernel(ids, a, b, c, d, mine, other):
    core = ids[0]

    def total(q):
        v = a[:, pl.ds(q, 1)].astype(F32) + b[:, pl.ds(q, 1)].astype(F32)
        v = v + (c[:, pl.ds(q, 1)].astype(F32) + d[:, pl.ds(q, 1)].astype(F32))
        return v.astype(BF)

    other[...] = total(1 - core)[:, 0]
    mine[...] = total(core)[:, 0]


def sum_parts(core, parts):
    nch = parts[0].shape[0]
    shape = jax.ShapeDtypeStruct((nch, 2, 128, S), BF)
    return pl.pallas_call(
        sum_kernel,
        in_specs=[pl.BlockSpec(memory_space=pltpu.SMEM)]
        + [pl.BlockSpec(memory_space=pltpu.VMEM)] * 4,
        out_specs=[pl.BlockSpec(memory_space=pltpu.VMEM)] * 2,
        out_shape=[shape, shape],
        compiler_params=pltpu.CompilerParams(vmem_limit_bytes=VMEM),
        cost_estimate=pl.CostEstimate(flops=1 << 20, bytes_accessed=5 << 18, transcendentals=0),
    )(core, *parts)


def right_kernel(ids, ranks, xm_ref, xo_ref, br_m, bi_m, br_o, bi_o, out_ref, *, lanes, chunk0):
    c = pl.program_id(0)
    g = pl.program_id(1)
    f = ids[0] * 2 + chunk0 + c

    def flip(v):
        return jnp.transpose(v.astype(F32), (1, 0))

    xr = jnp.concatenate([flip(xm_ref[0, 0]), flip(xo_ref[0, 0])], axis=1)
    xi = jnp.concatenate([flip(xm_ref[0, 1]), flip(xo_ref[0, 1])], axis=1)
    lhs = jnp.concatenate(
        [jnp.concatenate([xr, -xi], axis=1), jnp.concatenate([xi, xr], axis=1)], axis=0
    ).astype(BF)
    rhs = jnp.concatenate([br_m[0], br_o[0], bi_m[0], bi_o[0]], axis=0)
    acc = jnp.dot(lhs, rhs, preferred_element_type=F32)
    lane = lax.broadcasted_iota(jnp.int32, (S, 128), 1)
    low = lane < R
    kk = lane & (R - 1)
    for j in range(lanes // 128):
        tile = g * (lanes // R) + 2 * j
        even, odd = ranks[f * NB + tile], ranks[f * NB + tile + 1]
        re = acc[:S, j * 128 : (j + 1) * 128]
        im = acc[S:, j * 128 : (j + 1) * 128]
        a = jnp.where(low, re, pltpu.roll(im, R, 1))
        b = jnp.where(low, pltpu.roll(re, R, 1), im)
        out_ref[2 * j, 0] = jnp.where(kk < even, a, 0.0).astype(BF)
        out_ref[2 * j + 1, 0] = jnp.where(kk < odd, b, 0.0).astype(BF)


def right_product(core, ranks, mine, other, basis, basis_other, chunk0):
    nch = mine.shape[0]
    lanes = 1024
    groups = NB * R // lanes

    def spec_m(part):
        return pl.BlockSpec(
            (1, 128, lanes), lambda c, g, ids, rk: (ids[0] * 2 + chunk0 + c, 0, g + part * groups)
        )

    def spec_o(part):
        return pl.BlockSpec(
            (1, 128, lanes), lambda c, g, ids, rk: (chunk0 + c, 0, g + part * groups)
        )

    xspec = pl.BlockSpec((1, 2, 128, S), lambda c, g, ids, rk: (c, 0, 0, 0))

    def kern(*refs):
        right_kernel(*refs, lanes=lanes, chunk0=chunk0)

    return pl.pallas_call(
        kern,
        grid_spec=pltpu.PrefetchScalarGridSpec(
            num_scalar_prefetch=2,
            grid=(nch, groups),
            in_specs=[xspec, xspec, spec_m(0), spec_m(1), spec_o(0), spec_o(1)],
            out_specs=pl.BlockSpec((lanes // R, 1, S, 128), lambda c, g, ids, rk: (g, c, 0, 0)),
        ),
        out_shape=jax.ShapeDtypeStruct((NB, nch, S, 128), BF),
        compiler_params=pltpu.CompilerParams(vmem_limit_bytes=VMEM),
        cost_estimate=pl.CostEstimate(
            flops=nch * 2 * 256 * 512 * 2048, bytes_accessed=nch * 3 << 20, transcendentals=0
        ),
    )(core, ranks, mine, other, basis, basis, basis_other, basis_other)


def left_kernel(ids, c_ref, am_ref, ao_ref, ym_ref, yo_ref, stack):
    lane = lax.broadcasted_iota(jnp.int32, (S, 128), 1)
    low = lane < R
    for j in range(NB // 2):
        even, odd = c_ref[2 * j, 0], c_ref[2 * j + 1, 0]
        cols = slice(j * 128, (j + 1) * 128)
        stack[:S, cols] = jnp.where(low, even, pltpu.roll(odd, R, 1))
        stack[S:, cols] = jnp.where(low, pltpu.roll(even, R, 1), odd)
    half = NB * R
    dims = (((1,), (1,)), ((), ()))
    for a_ref, y_ref in ((ao_ref, yo_ref), (am_ref, ym_ref)):
        p = lax.dot_general(a_ref[0, :, :half], stack[...], dims, preferred_element_type=F32)
        q = lax.dot_general(a_ref[0, :, half:], stack[...], dims, preferred_element_type=F32)
        y_ref[0, 0] = (p[:, :S] - q[:, S:]).astype(BF)
        y_ref[0, 1] = (p[:, S:] + q[:, :S]).astype(BF)


def left_product(core, coupled, basis, basis_other, chunk0):
    nch = coupled.shape[1]
    yspec = pl.BlockSpec((1, 2, 128, S), lambda c, ids: (c, 0, 0, 0))
    shape = jax.ShapeDtypeStruct((nch, 2, 128, S), BF)
    return pl.pallas_call(
        left_kernel,
        grid_spec=pltpu.PrefetchScalarGridSpec(
            num_scalar_prefetch=1,
            grid=(nch,),
            in_specs=[
                pl.BlockSpec((NB, 1, S, 128), lambda c, ids: (0, c, 0, 0)),
                pl.BlockSpec((1, 128, 2 * NB * R), lambda c, ids: (ids[0] * 2 + chunk0 + c, 0, 0)),
                pl.BlockSpec((1, 128, 2 * NB * R), lambda c, ids: (chunk0 + c, 0, 0)),
            ],
            out_specs=[yspec, yspec],
            scratch_shapes=[pltpu.VMEM((2 * S, NB * R), BF)],
        ),
        out_shape=[shape, shape],
        compiler_params=pltpu.CompilerParams(vmem_limit_bytes=VMEM),
        cost_estimate=pl.CostEstimate(
            flops=nch * 2 * 256 * 4096 * 256, bytes_accessed=nch * 3 << 20, transcendentals=0
        ),
    )(core, coupled, basis, basis_other)


def swap(x):
    return lax.ppermute(x, "c", [(0, 1), (1, 0)])


def body(traces, right_basis, left_basis, tile_ranks):
    core = lax.axis_index("c").astype(jnp.int32)
    core_id = core.reshape(1)
    yid = lax.axis_index("y").astype(jnp.int32).reshape(1)
    chip = lax.axis_index("z") * NX + lax.axis_index("x")
    weights = jnp.asarray(twiddle_blocks())
    parts = dft(yid, weights, traces)
    ranks = lax.dynamic_slice_in_dim(tile_ranks, chip, 1, 2).reshape(FDEV * NB)
    arrived = [parts[0]]
    for d in range(1, NY):
        arrived.append(lax.ppermute(parts[d], "y", [(i, (i + d) % NY) for i in range(NY)]))
    right_other = swap(lax.dynamic_slice_in_dim(right_basis, 2 * (1 - core), 2, 0))
    left_other = swap(lax.dynamic_slice_in_dim(left_basis, 2 * (1 - core), 2, 0))
    mine, other = sum_parts(core_id, arrived)
    other = swap(other)
    outgoing = right_product(core_id, ranks, mine, other, right_basis, right_other, 0)
    coupled = lax.all_to_all(outgoing, ("z", "x"), split_axis=0, concat_axis=0, tiled=True)
    field, field_other = left_product(core_id, coupled, left_basis, left_other, 0)
    field_in = swap(field_other)
    return jnp.where(
        core == 0,
        jnp.concatenate([field, field_in], axis=0),
        jnp.concatenate([field_in, field], axis=0),
    )


def solution(mesh):
    inner = Mesh(mesh.devices.reshape(NY, NZ, NX, NC), ("y", "z", "x", "c"))
    tile = ("z", "x", "c")
    return jax.shard_map(
        body,
        mesh=inner,
        in_specs=(
            P("y", tile, None),
            P("y", tile, None),
            P("y", tile, None),
            P("y", None, None),
        ),
        out_specs=P("y", None, tile, None),
        check_vma=False,
    )
```

```python
import math

import jax
import jax.numpy as jnp
import numpy as np
from jax import lax
from jax.experimental import pallas as pl
from jax.experimental.pallas import tpu as pltpu
from jax.sharding import Mesh
from jax.sharding import PartitionSpec as P

N = 8192
TB = 256
R = 64
S = 128
NF = 16
NT = 256
NB = 32
NY, NZ, NX, NC = 4, 8, 4, 2
TROWS = NT // NY
FDEV = NF // NY
BF = jnp.bfloat16
F32 = jnp.float32
GROUP = 16
VMEM = 20 * 1024 * 1024
HBM = pltpu.MemorySpace.HBM


def in_hbm(x):
    return pltpu.with_memory_space_constraint(x, pltpu.MemorySpace.HBM)


def twiddle_blocks():
    k = np.arange(1, NF + 1)[:, None]
    t = np.arange(NT)[None, :]
    angle = ((k * t) % NT).astype(np.float32) * np.float32(2.0 * math.pi / NT)
    scale = np.float32(1.0 / math.sqrt(NT))
    tw = np.stack([np.cos(angle) * scale, -np.sin(angle) * scale], 1)
    tw = tw.reshape(NY, NC, 2, 2, NY, TROWS)
    out = np.zeros((NY, NY, 2, NC, 2, TROWS), np.float32)
    for y in range(NY):
        for d in range(NY):
            out[y, d] = np.transpose(tw[(y + d) % NY, :, :, :, y], (1, 0, 2, 3))
    out = out.reshape(NY, 32, TROWS)
    eye = np.eye(GROUP, dtype=np.float32)
    big = out[:, :, None, :, None] * eye[None, None, :, None, :]
    return big.reshape(NY, 32 * GROUP, TROWS * GROUP).astype(jnp.bfloat16)


def dft_kernel(ids, w_hbm, t_hbm, *refs):
    outs = refs[:NY]
    w_ref, t_ref, sem = refs[NY:]
    chunks = t_ref.shape[0]
    rows = t_ref.shape[2]
    w_copy = pltpu.make_async_copy(w_hbm.at[ids[0]], w_ref, sem.at[chunks])
    t_copies = [
        pltpu.make_async_copy(t_hbm.at[:, pl.ds(i * rows, rows), :], t_ref.at[i], sem.at[i])
        for i in range(chunks)
    ]
    w_copy.start()
    t_copies[0].start()
    w_copy.wait()
    t_copies[1].start()
    for i in range(chunks):
        t_copies[i].wait()
        if i + 2 < chunks:
            t_copies[i + 2].start()
        cols = [
            t_ref[i, :, g * GROUP : (g + 1) * GROUP, :].reshape(TROWS * GROUP, S)
            for g in range(rows // GROUP)
        ]
        acc = jnp.dot(w_ref[...], jnp.concatenate(cols, axis=1), preferred_element_type=F32)
        acc = acc.astype(BF)
        for o, ref in enumerate(outs):
            for j in range(8):
                row = (o * 8 + j) * GROUP
                for g in range(rows // GROUP):
                    base = i * rows + g * GROUP
                    ref[j // 4, (j // 2) % 2, j % 2, base : base + GROUP, :] = acc[
                        row : row + GROUP, g * S : (g + 1) * S
                    ]


def dft(ids, w, traces):
    chunks, rows = 4, 32
    hbm = pl.BlockSpec(memory_space=pl.ANY)
    return pl.pallas_call(
        dft_kernel,
        in_specs=[pl.BlockSpec(memory_space=pltpu.SMEM), hbm, hbm],
        out_specs=[pl.BlockSpec(memory_space=pltpu.VMEM)] * NY,
        out_shape=[jax.ShapeDtypeStruct((2, NC, 2, 128, S), BF)] * NY,
        scratch_shapes=[
            pltpu.VMEM((32 * GROUP, TROWS * GROUP), BF),
            pltpu.VMEM((chunks, TROWS, rows, S), BF),
            pltpu.SemaphoreType.DMA((chunks + 1,)),
        ],
        compiler_params=pltpu.CompilerParams(vmem_limit_bytes=VMEM),
        cost_estimate=pl.CostEstimate(
            flops=2 * 512 * 1024 * 1024, bytes_accessed=4 << 20, transcendentals=0
        ),
    )(ids, in_hbm(w), in_hbm(traces))


def sum_kernel(ids, a, b, c, d, mine, other):
    core = ids[0]

    def total(q):
        v = a[:, pl.ds(q, 1)].astype(F32) + b[:, pl.ds(q, 1)].astype(F32)
        v = v + (c[:, pl.ds(q, 1)].astype(F32) + d[:, pl.ds(q, 1)].astype(F32))
        return v.astype(BF)

    other[...] = total(1 - core)[:, 0]
    mine[...] = total(core)[:, 0]


def sum_parts(core, parts):
    nch = parts[0].shape[0]
    shape = jax.ShapeDtypeStruct((nch, 2, 128, S), BF)
    return pl.pallas_call(
        sum_kernel,
        in_specs=[pl.BlockSpec(memory_space=pltpu.SMEM)]
        + [pl.BlockSpec(memory_space=pltpu.VMEM)] * 4,
        out_specs=[pl.BlockSpec(memory_space=pltpu.VMEM)] * 2,
        out_shape=[shape, shape],
        compiler_params=pltpu.CompilerParams(vmem_limit_bytes=VMEM),
        cost_estimate=pl.CostEstimate(flops=1 << 20, bytes_accessed=5 << 18, transcendentals=0),
    )(core, *parts)


def right_kernel(
    ids, ranks, xm_ref, xo_ref, bm_hbm, bo_hbm, out_hbm, bm_ref, bo_ref, out_ref, lhs, sem, osem
):
    lanes = 1024
    tiles = lanes // R
    stages = [(c, g) for g in range(NB * R // lanes) for c in range(2)]
    copies = []
    for k, (c, g) in enumerate(stages):
        group = []
        for part in range(2):
            cols = pl.ds(part * NB * R + g * lanes, lanes)
            for i, (hbm, ref) in enumerate(((bm_hbm, bm_ref), (bo_hbm, bo_ref))):
                group.append(
                    pltpu.make_async_copy(
                        hbm.at[ids[0] * 2 + c, :, cols],
                        ref.at[c, :, cols],
                        sem.at[4 * k + 2 * part + i],
                    )
                )
        copies.append(group)
    for group in copies[:2]:
        for copy in group:
            copy.start()
    for c in range(2):
        xr = jnp.concatenate([xm_ref[c, 0].T, xo_ref[c, 0].T], axis=1)
        xi = jnp.concatenate([xm_ref[c, 1].T, xo_ref[c, 1].T], axis=1)
        lhs[c, :S] = jnp.concatenate([xr, -xi], axis=1)
        lhs[c, S:] = jnp.concatenate([xi, xr], axis=1)

    lane = lax.broadcasted_iota(jnp.int32, (1, 128), 1)
    low = lax.broadcasted_iota(jnp.int32, (S, 128), 1) < R
    kk = lane & (R - 1)
    outs = []
    for k, (c, g) in enumerate(stages):
        for copy in copies[k]:
            copy.wait()
        for copy in copies[k + 2] if k + 2 < len(stages) else []:
            copy.start()
        for h in range(tiles // 4):
            tile = g * tiles + 4 * h
            re_cols = slice(tile * R, tile * R + 256)
            im_cols = slice(NB * R + tile * R, NB * R + tile * R + 256)
            rhs = jnp.concatenate(
                [
                    bm_ref[c, :, re_cols],
                    bo_ref[c, :, re_cols],
                    bm_ref[c, :, im_cols],
                    bo_ref[c, :, im_cols],
                ],
                axis=0,
            )
            acc = jnp.dot(lhs[c], rhs, preferred_element_type=F32)
            base = (ids[0] * 2 + c) * NB + tile
            for j in range(2):
                keep = kk < jnp.where(lane < R, ranks[base + 2 * j], ranks[base + 2 * j + 1])
                re = jnp.where(keep, acc[:S, j * 128 : (j + 1) * 128], 0.0).astype(BF)
                im = jnp.where(keep, acc[S:, j * 128 : (j + 1) * 128], 0.0).astype(BF)
                out_ref[tile + 2 * j, c] = jnp.where(low, re, pltpu.roll(im, R, 1))
                out_ref[tile + 2 * j + 1, c] = jnp.where(low, pltpu.roll(re, R, 1), im)
        if c == 1:
            rows = pl.ds(g * tiles, tiles)
            outs.append(pltpu.make_async_copy(out_ref.at[rows], out_hbm.at[rows], osem.at[g]))
            outs[-1].start()
    for copy in outs:
        copy.wait()


def right_product(core, ranks, mine, other, basis, basis_other):
    whole = pl.BlockSpec(memory_space=pltpu.VMEM)
    smem = pl.BlockSpec(memory_space=pltpu.SMEM)
    hbm = pl.BlockSpec(memory_space=pl.ANY)
    half = (2,) + basis.shape[1:]
    shape = (NB, 2, S, 128)
    return pl.pallas_call(
        right_kernel,
        in_specs=[smem, smem, whole, whole, hbm, hbm],
        out_specs=hbm,
        out_shape=HBM(shape, BF),
        scratch_shapes=[
            pltpu.VMEM(half, BF),
            pltpu.VMEM(half, BF),
            pltpu.VMEM(shape, BF),
            pltpu.VMEM((2, 2 * S, 512), BF),
            pltpu.SemaphoreType.DMA((16,)),
            pltpu.SemaphoreType.DMA((2,)),
        ],
        compiler_params=pltpu.CompilerParams(vmem_limit_bytes=VMEM),
        cost_estimate=pl.CostEstimate(
            flops=2 * 2 * 256 * 512 * 2048, bytes_accessed=6 << 20, transcendentals=0
        ),
    )(core, ranks, mine, other, in_hbm(basis), in_hbm(basis_other))


def left_kernel(
    ids, c_ref, am_hbm, ao_hbm, ym_ref, yo_ref, am_ref, ao_ref, stack, sem
):
    half = NB * R
    width = half // 2
    per = NB // 2
    stages = [(c, g) for c in range(2) for g in range(2)]
    copies = []
    for k, (c, g) in enumerate(stages):
        group = []
        for part in range(2):
            cols = pl.ds(part * half + g * width, width)
            for i, (hbm, ref) in enumerate(((am_hbm, am_ref), (ao_hbm, ao_ref))):
                group.append(
                    pltpu.make_async_copy(
                        hbm.at[ids[0] * 2 + c, :, cols],
                        ref.at[c, :, cols],
                        sem.at[4 * k + 2 * part + i],
                    )
                )
        copies.append(group)
    for group in copies[:2]:
        for copy in group:
            copy.start()
    low = lax.broadcasted_iota(jnp.int32, (S, 128), 1) < R
    dims = (((1,), (1,)), ((), ()))
    total = None
    for k, (c, g) in enumerate(stages):
        for j in range(g * per // 2, (g + 1) * per // 2):
            even, odd = c_ref[2 * j, c], c_ref[2 * j + 1, c]
            cols = slice(j * 128, (j + 1) * 128)
            stack[c, :S, cols] = jnp.where(low, even, pltpu.roll(odd, R, 1))
            stack[c, S:, cols] = jnp.where(low, pltpu.roll(even, R, 1), odd)
        for copy in copies[k]:
            copy.wait()
        for copy in copies[k + 2] if k + 2 < len(stages) else []:
            copy.start()
        re_cols = slice(g * width, (g + 1) * width)
        im_cols = slice(half + g * width, half + (g + 1) * width)
        lhs = jnp.concatenate(
            [
                ao_ref[c, :, re_cols],
                am_ref[c, :, re_cols],
                ao_ref[c, :, im_cols],
                am_ref[c, :, im_cols],
            ],
            axis=0,
        )
        part = lax.dot_general(lhs, stack[c, :, re_cols], dims, preferred_element_type=F32)
        total = part if g == 0 else total + part
        if g == 1:
            for i, y_ref in enumerate((yo_ref, ym_ref)):
                p = total[i * 128 : (i + 1) * 128]
                q = total[256 + i * 128 : 256 + (i + 1) * 128]
                y_ref[c, 0] = (p[:, :S] - q[:, S:]).astype(BF)
                y_ref[c, 1] = (p[:, S:] + q[:, :S]).astype(BF)


def left_product(core, coupled, basis, basis_other):
    shape = jax.ShapeDtypeStruct((2, 2, 128, S), BF)
    whole = pl.BlockSpec(memory_space=pltpu.VMEM)
    hbm = pl.BlockSpec(memory_space=pl.ANY)
    half = (2,) + basis.shape[1:]
    return pl.pallas_call(
        left_kernel,
        in_specs=[pl.BlockSpec(memory_space=pltpu.SMEM), whole, hbm, hbm],
        out_specs=[whole] * 2,
        out_shape=[shape, shape],
        scratch_shapes=[
            pltpu.VMEM(half, BF),
            pltpu.VMEM(half, BF),
            pltpu.VMEM((2, 2 * S, NB * R), BF),
            pltpu.SemaphoreType.DMA((16,)),
        ],
        compiler_params=pltpu.CompilerParams(vmem_limit_bytes=VMEM),
        cost_estimate=pl.CostEstimate(
            flops=2 * 2 * 256 * 4096 * 256, bytes_accessed=6 << 20, transcendentals=0
        ),
    )(core, coupled, in_hbm(basis), in_hbm(basis_other))


def swap(x):
    return lax.ppermute(x, "c", [(0, 1), (1, 0)])


def body(traces, right_basis, left_basis, tile_ranks):
    core = lax.axis_index("c").astype(jnp.int32)
    core_id = core.reshape(1)
    yid = lax.axis_index("y").astype(jnp.int32)
    chip = lax.axis_index("z") * NX + lax.axis_index("x")
    weights = jnp.asarray(twiddle_blocks())
    parts = dft(yid.reshape(1), weights, traces)
    ranks = lax.dynamic_slice_in_dim(tile_ranks, chip, 1, 2).reshape(FDEV * NB)
    arrived = [parts[0]]
    for d in range(1, NY):
        arrived.append(lax.ppermute(parts[d], "y", [(i, (i + d) % NY) for i in range(NY)]))
    right_other = swap(right_basis)
    mine, other = sum_parts(core_id, arrived)
    other = swap(other)
    outgoing = right_product(core_id, ranks, mine, other, right_basis, right_other)
    coupled = lax.all_to_all(outgoing, ("z", "x"), split_axis=0, concat_axis=0, tiled=True)
    left_other = swap(left_basis)
    field, field_other = left_product(core_id, coupled, left_basis, left_other)
    field_in = swap(field_other)
    return jnp.where(
        core == 0,
        jnp.concatenate([field, field_in], axis=0),
        jnp.concatenate([field_in, field], axis=0),
    )


def solution(mesh):
    inner = Mesh(mesh.devices.reshape(NY, NZ, NX, NC), ("y", "z", "x", "c"))
    tile = ("z", "x", "c")
    return jax.shard_map(
        body,
        mesh=inner,
        in_specs=(
            P("y", tile, None),
            P("y", tile, None),
            P("y", tile, None),
            P("y", None, None),
        ),
        out_specs=P("y", None, tile, None),
        check_vma=False,
    )
```

```python
import math

import jax
import jax.numpy as jnp
import numpy as np
from jax import lax
from jax.experimental import pallas as pl
from jax.experimental.pallas import tpu as pltpu
from jax.sharding import Mesh
from jax.sharding import PartitionSpec as P

N = 8192
TB = 256
R = 64
S = 128
NF = 16
NT = 256
NB = 32
NY, NZ, NX, NC = 4, 8, 4, 2
TROWS = NT // NY
FDEV = NF // NY
BF = jnp.bfloat16
F32 = jnp.float32
GROUP = 16
VMEM = 20 * 1024 * 1024
HBM = pltpu.MemorySpace.HBM


def in_hbm(x):
    return pltpu.with_memory_space_constraint(x, pltpu.MemorySpace.HBM)


def twiddle_blocks():
    k = np.arange(1, NF + 1)[:, None]
    t = np.arange(NT)[None, :]
    angle = ((k * t) % NT).astype(np.float32) * np.float32(2.0 * math.pi / NT)
    scale = np.float32(1.0 / math.sqrt(NT))
    tw = np.stack([np.cos(angle) * scale, -np.sin(angle) * scale], 1)
    tw = tw.reshape(NY, NC, 2, 2, NY, TROWS)
    out = np.zeros((NY, NY, 2, NC, 2, TROWS), np.float32)
    for y in range(NY):
        for d in range(NY):
            out[y, d] = np.transpose(tw[(y + d) % NY, :, :, :, y], (1, 0, 2, 3))
    out = out.reshape(NY, 32, TROWS)
    eye = np.eye(GROUP, dtype=np.float32)
    big = out[:, :, None, :, None] * eye[None, None, :, None, :]
    return big.reshape(NY, 32 * GROUP, TROWS * GROUP).astype(jnp.bfloat16)


def dft_kernel(ids, w_hbm, t_hbm, *refs):
    outs = refs[:NY]
    w_ref, t_ref, sem = refs[NY:]
    chunks = t_ref.shape[0]
    rows = t_ref.shape[2]
    w_copy = pltpu.make_async_copy(w_hbm.at[ids[0]], w_ref, sem.at[chunks])
    t_copies = [
        pltpu.make_async_copy(t_hbm.at[:, pl.ds(i * rows, rows), :], t_ref.at[i], sem.at[i])
        for i in range(chunks)
    ]
    w_copy.start()
    for copy in t_copies:
        copy.start()
    w_copy.wait()
    for i in range(chunks):
        t_copies[i].wait()
        for pair in range(rows // (2 * GROUP)):
            cols = [
                t_ref[i, :, g * GROUP : (g + 1) * GROUP, :].reshape(TROWS * GROUP, S)
                for g in (2 * pair, 2 * pair + 1)
            ]
            acc = jnp.dot(w_ref[...], jnp.concatenate(cols, axis=1), preferred_element_type=F32)
            acc = acc.astype(BF)
            for o, ref in enumerate(outs):
                for j in range(8):
                    row = (o * 8 + j) * GROUP
                    for g in range(2):
                        base = i * rows + (2 * pair + g) * GROUP
                        ref[j // 4, (j // 2) % 2, j % 2, base : base + GROUP, :] = acc[
                            row : row + GROUP, g * S : (g + 1) * S
                        ]


def dft(ids, w, traces):
    chunks, rows = 2, 64
    hbm = pl.BlockSpec(memory_space=pl.ANY)
    return pl.pallas_call(
        dft_kernel,
        in_specs=[pl.BlockSpec(memory_space=pltpu.SMEM), hbm, hbm],
        out_specs=[pl.BlockSpec(memory_space=pltpu.VMEM)] * NY,
        out_shape=[jax.ShapeDtypeStruct((2, NC, 2, 128, S), BF)] * NY,
        scratch_shapes=[
            pltpu.VMEM((32 * GROUP, TROWS * GROUP), BF),
            pltpu.VMEM((chunks, TROWS, rows, S), BF),
            pltpu.SemaphoreType.DMA((chunks + 1,)),
        ],
        compiler_params=pltpu.CompilerParams(vmem_limit_bytes=VMEM),
        cost_estimate=pl.CostEstimate(
            flops=2 * 512 * 1024 * 1024, bytes_accessed=4 << 20, transcendentals=0
        ),
    )(ids, in_hbm(w), in_hbm(traces))


def sum_kernel(ids, a, b, c, d, mine, other):
    core = ids[0]

    def total(q):
        v = a[:, pl.ds(q, 1)].astype(F32) + b[:, pl.ds(q, 1)].astype(F32)
        v = v + (c[:, pl.ds(q, 1)].astype(F32) + d[:, pl.ds(q, 1)].astype(F32))
        return v.astype(BF)

    other[...] = total(1 - core)[:, 0]
    mine[...] = total(core)[:, 0]


def sum_parts(core, parts):
    nch = parts[0].shape[0]
    shape = jax.ShapeDtypeStruct((nch, 2, 128, S), BF)
    return pl.pallas_call(
        sum_kernel,
        in_specs=[pl.BlockSpec(memory_space=pltpu.SMEM)]
        + [pl.BlockSpec(memory_space=pltpu.VMEM)] * 4,
        out_specs=[pl.BlockSpec(memory_space=pltpu.VMEM)] * 2,
        out_shape=[shape, shape],
        compiler_params=pltpu.CompilerParams(vmem_limit_bytes=VMEM),
        cost_estimate=pl.CostEstimate(flops=1 << 20, bytes_accessed=5 << 18, transcendentals=0),
    )(core, *parts)


def right_kernel(
    ids, ranks, xm_ref, xo_ref, bm_hbm, bo_hbm, out_hbm, bm_ref, bo_ref, out_ref, lhs, sem, osem
):
    lanes = NB * R // 2
    copies = []
    for g in range(2):
        group = []
        for c in range(2):
            for part in range(2):
                cols = pl.ds(part * NB * R + g * lanes, lanes)
                for i, (hbm, ref) in enumerate(((bm_hbm, bm_ref), (bo_hbm, bo_ref))):
                    group.append(
                        pltpu.make_async_copy(
                            hbm.at[ids[0] * 2 + c, :, cols],
                            ref.at[c, :, cols],
                            sem.at[8 * g + 4 * c + 2 * part + i],
                        )
                    )
                    group[-1].start()
        copies.append(group)
    for c in range(2):
        xr = jnp.concatenate([xm_ref[c, 0].T, xo_ref[c, 0].T], axis=1)
        xi = jnp.concatenate([xm_ref[c, 1].T, xo_ref[c, 1].T], axis=1)
        lhs[c, :S] = jnp.concatenate([xr, -xi], axis=1)
        lhs[c, S:] = jnp.concatenate([xi, xr], axis=1)

    lane = lax.broadcasted_iota(jnp.int32, (1, 128), 1)
    low = lax.broadcasted_iota(jnp.int32, (S, 128), 1) < R
    kk = lane & (R - 1)
    outs = []
    for tile in range(0, NB, 4):
        if tile * R % lanes == 0:
            for copy in copies[tile * R // lanes]:
                copy.wait()
        re_cols = slice(tile * R, tile * R + 256)
        im_cols = slice(NB * R + tile * R, NB * R + tile * R + 256)
        for c in range(2):
            rhs = jnp.concatenate(
                [
                    bm_ref[c, :, re_cols],
                    bo_ref[c, :, re_cols],
                    bm_ref[c, :, im_cols],
                    bo_ref[c, :, im_cols],
                ],
                axis=0,
            )
            acc = jnp.dot(lhs[c], rhs, preferred_element_type=F32)
            base = (ids[0] * 2 + c) * NB + tile
            for j in range(2):
                keep = kk < jnp.where(lane < R, ranks[base + 2 * j], ranks[base + 2 * j + 1])
                re = jnp.where(keep, acc[:S, j * 128 : (j + 1) * 128], 0.0).astype(BF)
                im = jnp.where(keep, acc[S:, j * 128 : (j + 1) * 128], 0.0).astype(BF)
                out_ref[tile + 2 * j, c] = jnp.where(low, re, pltpu.roll(im, R, 1))
                out_ref[tile + 2 * j + 1, c] = jnp.where(low, pltpu.roll(re, R, 1), im)
        rows = pl.ds(tile, 4)
        outs.append(pltpu.make_async_copy(out_ref.at[rows], out_hbm.at[rows], osem.at[tile // 4]))
        outs[-1].start()
    for copy in outs:
        copy.wait()


def right_product(core, ranks, mine, other, basis, basis_other):
    whole = pl.BlockSpec(memory_space=pltpu.VMEM)
    smem = pl.BlockSpec(memory_space=pltpu.SMEM)
    hbm = pl.BlockSpec(memory_space=pl.ANY)
    half = (2,) + basis.shape[1:]
    shape = (NB, 2, S, 128)
    return pl.pallas_call(
        right_kernel,
        in_specs=[smem, smem, whole, whole, hbm, hbm],
        out_specs=hbm,
        out_shape=HBM(shape, BF),
        scratch_shapes=[
            pltpu.VMEM(half, BF),
            pltpu.VMEM(half, BF),
            pltpu.VMEM(shape, BF),
            pltpu.VMEM((2, 2 * S, 512), BF),
            pltpu.SemaphoreType.DMA((16,)),
            pltpu.SemaphoreType.DMA((8,)),
        ],
        compiler_params=pltpu.CompilerParams(vmem_limit_bytes=VMEM),
        cost_estimate=pl.CostEstimate(
            flops=2 * 2 * 256 * 512 * 2048, bytes_accessed=6 << 20, transcendentals=0
        ),
    )(core, ranks, mine, other, in_hbm(basis), in_hbm(basis_other))


def left_kernel(ids, c_ref, am_hbm, ao_hbm, ym_ref, yo_ref, am_ref, ao_ref, stack, sem):
    half = NB * R
    copies = []
    for c in range(2):
        group = []
        for i, (hbm, ref) in enumerate(((ao_hbm, ao_ref), (am_hbm, am_ref))):
            group.append(
                pltpu.make_async_copy(hbm.at[ids[0] * 2 + c], ref.at[c], sem.at[2 * c + i])
            )
            group[-1].start()
        copies.append(group)
    low = lax.broadcasted_iota(jnp.int32, (S, 128), 1) < R
    dims = (((1,), (1,)), ((), ()))
    for c in range(2):
        for j in range(NB // 2):
            even, odd = c_ref[2 * j, c], c_ref[2 * j + 1, c]
            cols = slice(j * 128, (j + 1) * 128)
            stack[c, :S, cols] = jnp.where(low, even, pltpu.roll(odd, R, 1))
            stack[c, S:, cols] = jnp.where(low, pltpu.roll(even, R, 1), odd)
    for c in range(2):
        for copy in copies[c]:
            copy.wait()
        for a_ref, y_ref in ((ao_ref, yo_ref), (am_ref, ym_ref)):
            lhs = jnp.concatenate([a_ref[c, :, :half], a_ref[c, :, half:]], axis=0)
            total = lax.dot_general(lhs, stack[c], dims, preferred_element_type=F32)
            p, q = total[:128], total[128:]
            y_ref[c, 0] = (p[:, :S] - q[:, S:]).astype(BF)
            y_ref[c, 1] = (p[:, S:] + q[:, :S]).astype(BF)


def left_product(core, coupled, basis, basis_other):
    shape = jax.ShapeDtypeStruct((2, 2, 128, S), BF)
    whole = pl.BlockSpec(memory_space=pltpu.VMEM)
    hbm = pl.BlockSpec(memory_space=pl.ANY)
    half = (2,) + basis.shape[1:]
    return pl.pallas_call(
        left_kernel,
        in_specs=[pl.BlockSpec(memory_space=pltpu.SMEM), whole, hbm, hbm],
        out_specs=[whole] * 2,
        out_shape=[shape, shape],
        scratch_shapes=[
            pltpu.VMEM(half, BF),
            pltpu.VMEM(half, BF),
            pltpu.VMEM((2, 2 * S, NB * R), BF),
            pltpu.SemaphoreType.DMA((4,)),
        ],
        compiler_params=pltpu.CompilerParams(vmem_limit_bytes=VMEM),
        cost_estimate=pl.CostEstimate(
            flops=2 * 2 * 256 * 4096 * 256, bytes_accessed=6 << 20, transcendentals=0
        ),
    )(core, coupled, in_hbm(basis), in_hbm(basis_other))


def swap(x):
    return lax.ppermute(x, "c", [(0, 1), (1, 0)])


def body(traces, right_basis, left_basis, tile_ranks):
    core = lax.axis_index("c").astype(jnp.int32)
    core_id = core.reshape(1)
    yid = lax.axis_index("y").astype(jnp.int32)
    chip = lax.axis_index("z") * NX + lax.axis_index("x")
    weights = jnp.asarray(twiddle_blocks())
    parts = dft(yid.reshape(1), weights, traces)
    ranks = lax.dynamic_slice_in_dim(tile_ranks, chip, 1, 2).reshape(FDEV * NB)
    arrived = [parts[0]] * NY
    for d in (2, 1, 3):
        arrived[d] = lax.ppermute(parts[d], "y", [(i, (i + d) % NY) for i in range(NY)])
    right_other = swap(right_basis)
    mine, other = sum_parts(core_id, arrived)
    other = swap(other)
    outgoing = right_product(core_id, ranks, mine, other, right_basis, right_other)
    coupled = lax.all_to_all(outgoing, ("z", "x"), split_axis=0, concat_axis=0, tiled=True)
    left_other = swap(left_basis)
    field, field_other = left_product(core_id, coupled, left_basis, left_other)
    field_in = swap(field_other)
    return jnp.where(
        core == 0,
        jnp.concatenate([field, field_in], axis=0),
        jnp.concatenate([field_in, field], axis=0),
    )


def solution(mesh):
    inner = Mesh(mesh.devices.reshape(NY, NZ, NX, NC), ("y", "z", "x", "c"))
    tile = ("z", "x", "c")
    return jax.shard_map(
        body,
        mesh=inner,
        in_specs=(
            P("y", tile, None),
            P("y", tile, None),
            P("y", tile, None),
            P("y", None, None),
        ),
        out_specs=P("y", None, tile, None),
        check_vma=False,
    )
```

```python
import math

import jax
import jax.numpy as jnp
import numpy as np
from jax import lax
from jax.experimental import pallas as pl
from jax.experimental.pallas import tpu as pltpu
from jax.sharding import Mesh
from jax.sharding import PartitionSpec as P

N = 8192
TB = 256
R = 64
S = 128
NF = 16
NT = 256
NB = 32
NY, NZ, NX, NC = 4, 8, 4, 2
TROWS = NT // NY
FDEV = NF // NY
BF = jnp.bfloat16
F32 = jnp.float32
GROUP = 16
VMEM = 20 * 1024 * 1024
HBM = pltpu.MemorySpace.HBM


def in_hbm(x):
    return pltpu.with_memory_space_constraint(x, pltpu.MemorySpace.HBM)


def twiddle_blocks():
    k = np.arange(1, NF + 1)[:, None]
    t = np.arange(NT)[None, :]
    angle = ((k * t) % NT).astype(np.float32) * np.float32(2.0 * math.pi / NT)
    scale = np.float32(1.0 / math.sqrt(NT))
    tw = np.stack([np.cos(angle) * scale, -np.sin(angle) * scale], 1)
    tw = tw.reshape(NY, NC, 2, 2, NY, TROWS)
    out = np.zeros((2, NY, NY, NC, 2, TROWS), np.float32)
    for y in range(NY):
        for d in range(NY):
            out[:, y, d] = np.transpose(tw[(y + d) % NY, :, :, :, y], (1, 0, 2, 3))
    out = out.reshape(2, NY, 16, TROWS)
    eye = np.eye(GROUP, dtype=np.float32)
    big = out[:, :, :, None, :, None] * eye[None, None, None, :, None, :]
    return big.reshape(2, NY, 16 * GROUP, TROWS * GROUP).astype(jnp.bfloat16)


def dft_kernel(ids, w_hbm, t_hbm, *refs):
    outs = refs[:NY]
    w_ref, t_ref, sem = refs[NY:]
    chunks = t_ref.shape[0]
    rows = t_ref.shape[2]
    w_copy = pltpu.make_async_copy(w_hbm.at[ids[0]], w_ref, sem.at[chunks])
    t_copies = [
        pltpu.make_async_copy(t_hbm.at[:, pl.ds(i * rows, rows), :], t_ref.at[i], sem.at[i])
        for i in range(chunks)
    ]
    w_copy.start()
    for copy in t_copies:
        copy.start()
    w_copy.wait()
    for i in range(chunks):
        t_copies[i].wait()
        for pair in range(rows // (2 * GROUP)):
            cols = [
                t_ref[i, :, g * GROUP : (g + 1) * GROUP, :].reshape(TROWS * GROUP, S)
                for g in (2 * pair, 2 * pair + 1)
            ]
            acc = jnp.dot(w_ref[...], jnp.concatenate(cols, axis=1), preferred_element_type=F32)
            acc = acc.astype(BF)
            for o, ref in enumerate(outs):
                for j in range(4):
                    row = (o * 4 + j) * GROUP
                    for g in range(2):
                        base = i * rows + (2 * pair + g) * GROUP
                        ref[j // 2, j % 2, base : base + GROUP, :] = acc[
                            row : row + GROUP, g * S : (g + 1) * S
                        ]


def dft(ids, w, traces):
    chunks, rows = 2, 64
    hbm = pl.BlockSpec(memory_space=pl.ANY)
    return pl.pallas_call(
        dft_kernel,
        in_specs=[pl.BlockSpec(memory_space=pltpu.SMEM), hbm, hbm],
        out_specs=[pl.BlockSpec(memory_space=pltpu.VMEM)] * NY,
        out_shape=[jax.ShapeDtypeStruct((NC, 2, 128, S), BF)] * NY,
        scratch_shapes=[
            pltpu.VMEM((16 * GROUP, TROWS * GROUP), BF),
            pltpu.VMEM((chunks, TROWS, rows, S), BF),
            pltpu.SemaphoreType.DMA((chunks + 1,)),
        ],
        compiler_params=pltpu.CompilerParams(vmem_limit_bytes=VMEM),
        cost_estimate=pl.CostEstimate(
            flops=2 * 256 * 1024 * 1024, bytes_accessed=4 << 20, transcendentals=0
        ),
    )(ids, in_hbm(w), in_hbm(traces))


def sum_kernel(ids, a, b, c, d, *refs):
    mine, other = refs[-2:]
    core = ids[0]

    def total(q):
        v = a[pl.ds(q, 1)].astype(F32) + b[pl.ds(q, 1)].astype(F32)
        v = v + (c[pl.ds(q, 1)].astype(F32) + d[pl.ds(q, 1)].astype(F32))
        return v.astype(BF)

    other[...] = total(1 - core)
    mine[...] = total(core)


def sum_parts(core, parts, after):
    shape = jax.ShapeDtypeStruct((1, 2, 128, S), BF)
    return pl.pallas_call(
        sum_kernel,
        in_specs=[pl.BlockSpec(memory_space=pltpu.SMEM)]
        + [pl.BlockSpec(memory_space=pltpu.VMEM)] * (4 + len(after)),
        out_specs=[pl.BlockSpec(memory_space=pltpu.VMEM)] * 2,
        out_shape=[shape, shape],
        compiler_params=pltpu.CompilerParams(vmem_limit_bytes=VMEM),
        cost_estimate=pl.CostEstimate(flops=1 << 20, bytes_accessed=5 << 18, transcendentals=0),
    )(core, *parts, *after)


def first_kernel(ids, ranks, xm_ref, xo_ref, bm_hbm, bo_hbm, out_hbm, token, next_ref, *refs):
    b_ref, out_ref, lhs, sem, osem = refs
    token[...] = jnp.zeros_like(token)
    copies = []
    for c, ref in enumerate((b_ref, next_ref)):
        for i, hbm in enumerate((bm_hbm, bo_hbm)):
            copies.append(
                pltpu.make_async_copy(hbm.at[ids[0] * 2 + c], ref.at[i], sem.at[2 * c + i])
            )
    for copy in copies:
        copy.start()
    for copy in copies[:2]:
        copy.wait()
    one_product(ids, ranks, xm_ref, xo_ref, b_ref, out_hbm, out_ref, lhs, osem, 0)
    for copy in copies[2:]:
        copy.wait()


def second_kernel(ids, ranks, xm_ref, xo_ref, b_ref, earlier, out_hbm, out_ref, lhs, osem):
    one_product(ids, ranks, xm_ref, xo_ref, b_ref, out_hbm, out_ref, lhs, osem, 1)


def one_product(ids, ranks, xm_ref, xo_ref, b_ref, out_hbm, out_ref, lhs, osem, c):
    f = ids[0] * 2 + c
    xr = jnp.concatenate([xm_ref[0, 0].T, xo_ref[0, 0].T], axis=1)
    xi = jnp.concatenate([xm_ref[0, 1].T, xo_ref[0, 1].T], axis=1)
    lhs[:S] = jnp.concatenate([xr, -xi], axis=1)
    lhs[S:] = jnp.concatenate([xi, xr], axis=1)

    lane = lax.broadcasted_iota(jnp.int32, (1, 128), 1)
    low = lax.broadcasted_iota(jnp.int32, (S, 128), 1) < R
    kk = lane & (R - 1)
    outs = []
    for tile in range(0, NB, 4):
        re_cols = slice(tile * R, tile * R + 256)
        im_cols = slice(NB * R + tile * R, NB * R + tile * R + 256)
        rhs = jnp.concatenate(
            [b_ref[0, :, re_cols], b_ref[1, :, re_cols], b_ref[0, :, im_cols], b_ref[1, :, im_cols]],
            axis=0,
        )
        acc = jnp.dot(lhs[...], rhs, preferred_element_type=F32)
        base = f * NB + tile
        for j in range(2):
            keep = kk < jnp.where(lane < R, ranks[base + 2 * j], ranks[base + 2 * j + 1])
            re = jnp.where(keep, acc[:S, j * 128 : (j + 1) * 128], 0.0).astype(BF)
            im = jnp.where(keep, acc[S:, j * 128 : (j + 1) * 128], 0.0).astype(BF)
            out_ref[tile + 2 * j] = jnp.where(low, re, pltpu.roll(im, R, 1))
            out_ref[tile + 2 * j + 1] = jnp.where(low, pltpu.roll(re, R, 1), im)
        if tile % 8 == 4:
            rows = pl.ds(tile - 4, 8)
            outs.append(
                pltpu.make_async_copy(out_ref.at[rows], out_hbm.at[rows, c], osem.at[tile // 8])
            )
            outs[-1].start()
    for copy in outs:
        copy.wait()


def right_product(core, ranks, mine, other, bases, earlier):
    whole = pl.BlockSpec(memory_space=pltpu.VMEM)
    smem = pl.BlockSpec(memory_space=pltpu.SMEM)
    hbm = pl.BlockSpec(memory_space=pl.ANY)
    half = (2, 128, 2 * NB * R)
    work = [
        pltpu.VMEM((NB, S, 128), BF),
        pltpu.VMEM((2 * S, 512), BF),
    ]
    out = HBM((NB, 2, S, 128), BF)
    first = earlier is None
    options = dict(
        compiler_params=pltpu.CompilerParams(vmem_limit_bytes=VMEM),
        cost_estimate=pl.CostEstimate(
            flops=2 * 256 * 512 * 2048, bytes_accessed=3 << 20, transcendentals=0
        ),
    )
    if first:
        return pl.pallas_call(
            first_kernel,
            in_specs=[smem, smem, whole, whole, hbm, hbm],
            out_specs=[hbm, whole, whole],
            out_shape=[
                out,
                jax.ShapeDtypeStruct((8, 128), F32),
                jax.ShapeDtypeStruct(half, BF),
            ],
            scratch_shapes=[pltpu.VMEM(half, BF)]
            + work
            + [pltpu.SemaphoreType.DMA((4,)), pltpu.SemaphoreType.DMA((4,))],
            **options,
        )(core, ranks, mine, other, *[in_hbm(b) for b in bases])
    return pl.pallas_call(
        second_kernel,
        in_specs=[smem, smem, whole, whole, whole, hbm],
        out_specs=hbm,
        out_shape=out,
        input_output_aliases={5: 0},
        scratch_shapes=work + [pltpu.SemaphoreType.DMA((4,))],
        **options,
    )(core, ranks, mine, other, bases, in_hbm(earlier))


def left_kernel(ids, c_ref, am_hbm, ao_hbm, ym_ref, yo_ref, am_ref, ao_ref, stack, sem):
    half = NB * R
    copies = []
    for c in range(2):
        group = []
        for i, (source, ref) in enumerate(
            ((ao_hbm.at[c], ao_ref), (am_hbm.at[ids[0] * 2 + c], am_ref))
        ):
            group.append(pltpu.make_async_copy(source, ref.at[c], sem.at[2 * c + i]))
            group[-1].start()
        copies.append(group)
    low = lax.broadcasted_iota(jnp.int32, (S, 128), 1) < R
    dims = (((1,), (1,)), ((), ()))
    for c in range(2):
        for j in range(NB // 2):
            even, odd = c_ref[2 * j, c], c_ref[2 * j + 1, c]
            cols = slice(j * 128, (j + 1) * 128)
            stack[c, :S, cols] = jnp.where(low, even, pltpu.roll(odd, R, 1))
            stack[c, S:, cols] = jnp.where(low, pltpu.roll(even, R, 1), odd)
    for c in range(2):
        for copy in copies[c]:
            copy.wait()
        for a_ref, y_ref in ((ao_ref, yo_ref), (am_ref, ym_ref)):
            lhs = jnp.concatenate([a_ref[c, :, :half], a_ref[c, :, half:]], axis=0)
            total = lax.dot_general(lhs, stack[c], dims, preferred_element_type=F32)
            p, q = total[:128], total[128:]
            y_ref[c, 0] = (p[:, :S] - q[:, S:]).astype(BF)
            y_ref[c, 1] = (p[:, S:] + q[:, :S]).astype(BF)


def left_product(core, coupled, basis, basis_other):
    shape = jax.ShapeDtypeStruct((2, 2, 128, S), BF)
    whole = pl.BlockSpec(memory_space=pltpu.VMEM)
    hbm = pl.BlockSpec(memory_space=pl.ANY)
    half = (2,) + basis.shape[1:]
    return pl.pallas_call(
        left_kernel,
        in_specs=[pl.BlockSpec(memory_space=pltpu.SMEM), whole, hbm, hbm],
        out_specs=[whole] * 2,
        out_shape=[shape, shape],
        scratch_shapes=[
            pltpu.VMEM(half, BF),
            pltpu.VMEM(half, BF),
            pltpu.VMEM((2, 2 * S, NB * R), BF),
            pltpu.SemaphoreType.DMA((4,)),
        ],
        compiler_params=pltpu.CompilerParams(vmem_limit_bytes=VMEM),
        cost_estimate=pl.CostEstimate(
            flops=2 * 2 * 256 * 4096 * 256, bytes_accessed=6 << 20, transcendentals=0
        ),
    )(core, coupled, in_hbm(basis), in_hbm(basis_other))


def swap(x):
    return lax.ppermute(x, "c", [(0, 1), (1, 0)])


def body(traces, right_basis, left_basis, tile_ranks):
    core = lax.axis_index("c").astype(jnp.int32)
    core_id = core.reshape(1)
    yid = lax.axis_index("y").astype(jnp.int32)
    chip = lax.axis_index("z") * NX + lax.axis_index("x")
    weights = twiddle_blocks()
    ranks = lax.dynamic_slice_in_dim(tile_ranks, chip, 1, 2).reshape(FDEV * NB)
    right_other = swap(right_basis)
    arrived = []
    for c in range(2):
        parts = dft(yid.reshape(1), jnp.asarray(weights[c]), traces)
        chunk = [parts[0]] * NY
        for d in (2, 1, 3):
            chunk[d] = lax.ppermute(parts[d], "y", [(i, (i + d) % NY) for i in range(NY)])
        arrived.append(chunk)
    mine, other = sum_parts(core_id, arrived[0], [])
    outgoing, token, staged = right_product(
        core_id, ranks, mine, swap(other), (right_basis, right_other), None
    )
    mine, other = sum_parts(core_id, arrived[1], [token])
    outgoing = right_product(core_id, ranks, mine, swap(other), staged, outgoing)
    coupled = lax.all_to_all(
        outgoing, ("z", "x"), split_axis=0, concat_axis=0, tiled=True
    )
    left_other = swap(lax.dynamic_slice_in_dim(left_basis, 2 * (1 - core), 2, 0))
    field, field_other = left_product(core_id, coupled, left_basis, left_other)
    field_in = swap(field_other)
    return jnp.where(
        core == 0,
        jnp.concatenate([field, field_in], axis=0),
        jnp.concatenate([field_in, field], axis=0),
    )


def solution(mesh):
    inner = Mesh(mesh.devices.reshape(NY, NZ, NX, NC), ("y", "z", "x", "c"))
    tile = ("z", "x", "c")
    return jax.shard_map(
        body,
        mesh=inner,
        in_specs=(
            P("y", tile, None),
            P("y", tile, None),
            P("y", tile, None),
            P("y", None, None),
        ),
        out_specs=P("y", None, tile, None),
        check_vma=False,
    )
```
